256 devices in a mesh: blk: 32 (over x_lo, z, core), aux: 8 (over y, x_hi).
Axes of the slice: x: 4 (x_hi: 2, x_lo: 2; x = x_hi * 2 + x_lo), y: 4, z: 8, core: 2. Of those that a mesh axis runs over, the one named last changes fastest.
Arguments:
- factors: bfloat16 [128, 8192, 1024], P('aux', 'blk'), may hold values from -0.31445312 to 0.31445312
Outputs:
- exchange_band: float32 [8192, 4, 256], P('blk', None, 'aux')
The draws below stay inside these ranges and needn't reach their ends.
All inputs are finite; a program needn't handle non-finite values.
Results may differ from the reference program's by a relative error of at most 0.0003.
Values may be sent and summed in bfloat16 or wider, within the bound.
No kernel may reach another device: no remote copies, remote signals or barrier semaphores. Data moves between devices by JAX's collectives and lax.ppermute only.
A program may use at most 128 MiB of HBM per device.

```python
import jax
import jax.numpy as jnp
from jax import lax

NBF = 8192
NOCC = 1024
Q_DEV = 16
STEPS = 4
NAUX = 128
RB = 256
N_BLK = 32
N_AUX = 8


def levels(stream_key, shape, shards, smallest, high):
    loudness = 1.0
    for dim, shards_of in shards:
        steps = jax.random.uniform(jax.random.fold_in(jax.random.fold_in(stream_key, 6), dim), (shards_of,), jnp.float32, smallest / len(shards), high / len(shards))
        loudness = loudness * jnp.repeat(jnp.exp(steps), shape[dim] // shards_of).reshape((-1,) + (1,) * (len(shape) - 1 - dim))
    return loudness


def centred(own_key, shape, spread, bound, split=(), held_as=jnp.bfloat16):
    gain = levels(own_key, shape, split, -0.22, 0.18) if split else 1.0
    values = jax.random.normal(own_key, shape, jnp.float32) * spread * gain
    return jnp.minimum(jnp.maximum(values, -bound), bound).astype(held_as)


def setup_inputs(seed: int = 0) -> dict:
    splits = jax.random.split(jax.random.key(seed), 2)
    factors = centred(splits[0], (NAUX, NBF, NOCC), ((Q_DEV * N_AUX * NOCC) ** -0.25), 0.31445312, ((0, 8), (1, 32)))
    return dict(factors=factors)


def reference(factors):
    blocks = factors.reshape(NAUX, N_BLK, RB, NOCC)

    def one_block(index):
        own = lax.dynamic_index_in_dim(blocks, index, 1, keepdims=False).astype(jnp.float32)
        tiles = []
        for step in range(STEPS):
            other_index = ((index - step) % N_BLK).astype(jnp.int32)
            other = lax.dynamic_index_in_dim(blocks, other_index, 1, keepdims=False).astype(jnp.float32)
            tiles.append(lax.dot_general(own, other, (((0, 2), (0, 2)), ((), ())), preferred_element_type=jnp.float32))
        return jnp.stack(tiles, axis=1)

    result = lax.map(one_block, jnp.arange(N_BLK, dtype=jnp.int32))
    return result.reshape(NBF, STEPS, RB)
```

```python
import jax
import jax.numpy as jnp
from jax import lax
from jax.sharding import PartitionSpec as P

COUNT = 32
HALF = 8
SLICES = 8

TO_MATE = [(b, b ^ 1) for b in range(COUNT)]
TO_NEAR = [(b, (b - 1 if b % 2 == 0 else b + 1) % COUNT) for b in range(COUNT)]
FROM_FAR_NEAR = [(b, (b + 2 if b % 2 == 0 else b - 2) % COUNT) for b in range(COUNT)]
FROM_FAR_MATE = [(b, (b - 2 if b % 2 == 0 else b + 2) % COUNT) for b in range(COUNT)]
UP_ONE = [(b, (b + 1) % COUNT) for b in range(COUNT)]
UP_TWO = [(b, (b + 2) % COUNT) for b in range(COUNT)]
LAST_EVEN = [(b, (b + 2) % COUNT) for b in range(0, COUNT, 2)]
LAST_ODD = [(b, (b + 1) % COUNT) for b in range(1, COUNT, 2)]


def send(value, pairs):
    return lax.ppermute(value, "blk", pairs)


def contract(one, other):
    return lax.dot_general(
        one, other, (((0, 2), (0, 2)), ((), ())), preferred_element_type=jnp.float32
    )


def reduced(tiles):
    count = len(tiles)
    parts = jnp.stack(tiles).reshape(count, SLICES, 32, 256).transpose(1, 0, 2, 3)
    parts = lax.all_to_all(parts, "aux", 0, 0)
    return parts.sum(0)


def local(factors):
    odd = lax.axis_index("blk") % 2
    is_odd = odd == 1
    own = lax.dynamic_slice_in_dim(factors, odd * HALF, HALF, 0)
    rest = lax.dynamic_slice_in_dim(factors, (1 - odd) * HALF, HALF, 0)
    near = send(rest, TO_NEAR)
    mate = send(rest, TO_MATE)
    far_near = send(own, FROM_FAR_NEAR)
    far_mate = send(own, FROM_FAR_MATE)

    def oriented(one, other):
        tile = contract(one, other)
        return jnp.where(is_odd, tile.T, tile)

    first = reduced([contract(own, own), contract(mate, mate), oriented(own, mate)])
    own_own, mate_mate, own_mate = first[0], first[1], first[2]
    second = reduced(
        [oriented(near, own), oriented(near, mate), oriented(far_near, own), oriented(far_near, mate)]
    )
    near_own, near_mate, far_own, far_mate_ = second[0], second[1], second[2], second[3]

    zero = jnp.zeros_like(own_own)
    pick = lambda even, odd_: jnp.where(is_odd, odd_, even)
    from_mate = send(mate_mate, TO_MATE)
    from_below = send(
        jnp.stack([pick(own_mate, near_own), near_mate, pick(far_mate_, zero)]), UP_ONE
    )
    from_two = send(
        jnp.stack([pick(zero, far_own), pick(zero, far_mate_)]), UP_TWO
    )
    s0 = own_own + from_mate
    s1 = pick(near_own, own_mate) + from_below[0]
    s2 = pick(far_own, zero) + from_below[1] + from_two[0]
    s3 = from_below[2] + from_two[1]

    near, s3 = lax.optimization_barrier((near, s3))
    last = reduced([oriented(near, far_mate)])[0]
    s3 = s3 + send(last, LAST_EVEN) + send(last, LAST_ODD)
    return jnp.stack([s0, s1, s2, s3]).transpose(2, 0, 1)


def solution(mesh):
    placed = (P("aux", "blk", None),)
    return jax.shard_map(
        local, mesh=mesh, in_specs=placed, out_specs=P("blk", None, "aux"), check_vma=False
    )
```

```python
import functools

import jax
import jax.numpy as jnp
from jax import lax
from jax.experimental import pallas as pl
from jax.experimental.pallas import tpu as pltpu
from jax.sharding import PartitionSpec as P

COUNT = 32
HALF = 8
CUT = 6
ROWS = 256
DEPTH = 1024
F32 = jnp.float32
BF16 = jnp.bfloat16
ANY = pl.BlockSpec(memory_space=pl.ANY)
HBM = pl.BlockSpec(memory_space=pltpu.HBM)
VMEM = pl.BlockSpec(memory_space=pltpu.VMEM)

TO_MATE = [(b, b ^ 1) for b in range(COUNT)]
TO_NEAR = [(b, (b - 1 if b % 2 == 0 else b + 1) % COUNT) for b in range(COUNT)]
TO_FAR_NEAR = [(b, (b + 2 if b % 2 == 0 else b - 2) % COUNT) for b in range(COUNT)]
TO_FAR_MATE = [(b, (b - 2 if b % 2 == 0 else b + 2) % COUNT) for b in range(COUNT)]
EVEN_UP = [(b, (b + 2) % COUNT) for b in range(0, COUNT, 2)]


def along_y(shift):
    return [(a, ((a // 2 + shift) % 4) * 2 + a % 2) for a in range(8)]


ACROSS_X = [(a, a ^ 1) for a in range(8)]


def to_upper_even(flip):
    pairs = []
    for b in range(COUNT):
        core = b % 2
        for y in range(4):
            source, target = 2 * y + (core ^ flip), 2 * y + core
            pairs.append((b * 8 + source, (b - core + 2) % COUNT * 8 + target))
    return pairs


def f32(*shape):
    return jax.ShapeDtypeStruct(shape, F32)


def parity():
    return lax.rem(lax.axis_index("blk"), 2)


def call(kernel, out_shape, *args, flops=0, scratch=(), specs=None, hidden=(), limit=16):
    single = not isinstance(out_shape, list)
    moved = sum(a.size * a.dtype.itemsize for a in args)
    return pl.pallas_call(
        kernel,
        out_shape=out_shape,
        in_specs=(specs or [VMEM] * len(args)) + [ANY] * len(hidden),
        out_specs=VMEM if single else [VMEM] * len(out_shape),
        scratch_shapes=list(scratch),
        compiler_params=pltpu.CompilerParams(vmem_limit_bytes=limit << 20),
        cost_estimate=pl.CostEstimate(flops=flops, bytes_accessed=moved, transcendentals=0),
    )(*args, *hidden)


def take_kernel(other, first, count, factors, *refs):
    out, sems = refs[-2:]
    odd = parity()
    base = (1 - odd if other else odd) * HALF + first
    copies = [
        pltpu.make_async_copy(factors.at[base + i], out.at[i], sems.at[i]) for i in range(count)
    ]
    for copy in copies:
        copy.start()
    for copy in copies:
        copy.wait()


def take(factors, other, first, count, after=(), limit=16):
    return call(
        functools.partial(take_kernel, other, first, count),
        jax.ShapeDtypeStruct((count, ROWS, DEPTH), BF16),
        factors,
        scratch=[pltpu.SemaphoreType.DMA((count,))],
        specs=[HBM],
        hidden=after,
        limit=limit,
    )


def dot(lo, hi):
    return lax.dot_general(lo, hi, (((1,), (1,)), ((), ())), preferred_element_type=F32)


def accumulate(totals, pairs, first=0, last=HALF):
    totals[...] = jnp.zeros(totals.shape, F32)
    cuts = {first, last}
    for pair in pairs:
        for operand in pair:
            cuts |= {at for _, at in operand if first < at < last}
    cuts = sorted(cuts)

    def holder(operand, at):
        return [piece for piece in operand if piece[1] <= at][-1]

    for low, high in zip(cuts, cuts[1:]):
        held = [[holder(operand, low) for operand in pair] for pair in pairs]

        def step(q, carry):
            for t, ((lo, lo_at), (hi, hi_at)) in enumerate(held):
                totals[t] += dot(lo[q - lo_at], hi[q - hi_at])
            return carry

        lax.fori_loop(low, high, step, 0)


def by_parity(even, odd):
    for which, action in ((0, even), (1, odd)):
        pl.when(parity() == which)(action)


def row_of(shift, height):
    y = lax.div(lax.axis_index("aux"), 2)
    return pl.multiple_of(lax.rem(y + shift, 4) * height, height)


def spread(totals, outs):
    for shift, out in enumerate(outs):
        out[...] = totals[:, pl.ds(row_of(shift, 64), 64)]


def chip_kernel(own0, own1, mate0, *refs):
    outs, totals = refs[:4], refs[4]
    own, mate = [(own0, 0), (own1, CUT)], [(mate0, 0)]
    by_parity(
        lambda: accumulate(totals, [(own, own), (mate, mate), (own, mate)]),
        lambda: accumulate(totals, [(mate, mate), (own, own), (mate, own)]),
    )
    spread(totals, outs)


def window_kernel(own0, own1, mate0, near0, far0, far1, hidden, *refs):
    outs, totals = refs[:4], refs[4]
    own, far = [(own0, 0), (own1, CUT)], [(far0, 0), (far1, CUT)]
    mate, near = [(mate0, 0)], [(near0, 0)]
    by_parity(
        lambda: accumulate(totals, [(near, own), (near, mate), (far, own), (far, mate)]),
        lambda: accumulate(totals, [(own, near), (own, far), (mate, near), (mate, far)]),
    )
    spread(totals, outs)


def sum_kernel(a, b, c, d, total):
    total[...] = a[...] + b[...] + c[...] + d[...]


def choose_kernel(chip, swapped, lower, keep, give):
    def even():
        keep[0] = chip[0]
        keep[1] = lower[0]
        keep[2] = lower[2]
        keep[3] = jnp.zeros((64, ROWS), F32)
        give[0:2] = chip[1:3]
        give[2] = lower[1]
        give[3] = lower[3]

    def odd():
        keep[0:2] = chip[1:3]
        keep[2] = swapped[1]
        keep[3] = swapped[3]
        give[0] = chip[0]
        give[1] = swapped[0]
        give[2] = swapped[2]
        give[3] = jnp.zeros((64, ROWS), F32)

    by_parity(even, odd)


def split_kernel(keep, given, stay, leave):
    pair = lax.rem(lax.axis_index("aux"), 2)
    for half, out in ((pair, stay), (1 - pair, leave)):
        rows = pl.ds(pl.multiple_of(32 * half, 32), 32)
        out[...] = keep[:, rows] + given[:, rows]


def early_kernel(near0, far0, hidden, total):
    near, far = [(near0, 0)], [(far0, 0)]
    by_parity(
        lambda: accumulate(total, [(near, far)], 0, CUT),
        lambda: accumulate(total, [(far, near)], 0, CUT),
    )


def last_kernel(near0, far1, early, keep, give, total):
    near, far = [(near0, 0)], [(far1, CUT)]
    by_parity(
        lambda: accumulate(total, [(near, far)], CUT, HALF),
        lambda: accumulate(total, [(far, near)], CUT, HALF),
    )
    core = parity()
    for y in range(4):
        for half, out in ((core, keep), (1 - core, give)):
            rows = pl.ds(pl.multiple_of(64 * y + 32 * half, 32), 32)
            out[32 * y : 32 * y + 32] = early[0, rows] + total[0, rows]


def combine_last_kernel(keep, given, *outs):
    for shift, out in enumerate(outs):
        rows = pl.ds(row_of(shift, 32), 32)
        out[...] = keep[rows] + given[rows]


def finish_kernel(stay, come, a, b, out):
    out[0:3] = stay[0:3] + come[0:3]
    out[3] = (stay[3] + come[3]) + (a[...] + b[...])


def sum_along_y(parts):
    return [parts[0]] + [lax.ppermute(parts[d], "aux", along_y(d)) for d in (1, 2, 3)]


def local(factors):
    def send(value, pairs):
        return lax.ppermute(value, "blk", pairs)

    tile = 2 * ROWS * ROWS * DEPTH
    rest = take(factors, True, 0, HALF)
    near = send(rest, TO_NEAR)
    own = [
        take(factors, False, 0, CUT, (rest,)),
        take(factors, False, CUT, HALF - CUT, (rest,)),
    ]
    far_near = [send(part, TO_FAR_NEAR) for part in own]
    far_mate = [send(part, TO_FAR_MATE) for part in own]
    mate = send(take(factors, True, 0, HALF, own), TO_MATE)

    parts = call(
        chip_kernel,
        [f32(3, 64, ROWS)] * 4,
        *own,
        mate,
        flops=3 * tile * HALF,
        scratch=[pltpu.VMEM((3, ROWS, ROWS), F32)],
    )
    chip = call(sum_kernel, f32(3, 64, ROWS), *sum_along_y(parts))
    parts = call(
        window_kernel,
        [f32(4, 64, ROWS)] * 4,
        *own,
        mate,
        near,
        *far_near,
        hidden=(chip,),
        flops=4 * tile * HALF,
        scratch=[pltpu.VMEM((4, ROWS, ROWS), F32)],
    )
    window = call(sum_kernel, f32(4, 64, ROWS), *sum_along_y(parts))
    swapped = send(window, TO_MATE)
    lower = send(swapped, EVEN_UP)
    keep, give = call(choose_kernel, [f32(4, 64, ROWS)] * 2, chip, swapped, lower)
    given = send(give, TO_MATE)

    stay, leave = call(split_kernel, [f32(4, 32, ROWS)] * 2, keep, given)
    come = lax.ppermute(leave, "aux", ACROSS_X)

    early = call(
        early_kernel, f32(1, ROWS, ROWS), near, far_mate[0], flops=CUT * tile, hidden=(leave,)
    )
    keep_last, give_last = call(
        last_kernel,
        [f32(128, ROWS)] * 2,
        near,
        far_mate[1],
        early,
        flops=(HALF - CUT) * tile,
        scratch=[pltpu.VMEM((1, ROWS, ROWS), F32)],
    )
    parts = call(combine_last_kernel, [f32(32, ROWS)] * 4, keep_last, send(give_last, TO_MATE))
    last = call(sum_kernel, f32(32, ROWS), *sum_along_y(parts))
    arrived = [lax.ppermute(last, ("blk", "aux"), to_upper_even(flip)) for flip in (1, 0)]
    out = call(finish_kernel, f32(4, 32, ROWS), stay, come, *arrived)
    return out.transpose(2, 0, 1)


def solution(mesh):
    placed = (P("aux", "blk", None),)
    return jax.shard_map(
        local, mesh=mesh, in_specs=placed, out_specs=P("blk", None, "aux"), check_vma=False
    )
```

```python
import functools

import jax
import jax.numpy as jnp
from jax import lax
from jax.experimental import pallas as pl
from jax.experimental.pallas import tpu as pltpu
from jax.sharding import PartitionSpec as P

COUNT = 32
HALF = 8
CUT = 7
ROWS = 256
DEPTH = 1024
F32 = jnp.float32
BF16 = jnp.bfloat16
ANY = pl.BlockSpec(memory_space=pl.ANY)
HBM = pl.BlockSpec(memory_space=pltpu.HBM)
VMEM = pl.BlockSpec(memory_space=pltpu.VMEM)

TO_MATE = [(b, b ^ 1) for b in range(COUNT)]
TO_NEAR = [(b, (b - 1 if b % 2 == 0 else b + 1) % COUNT) for b in range(COUNT)]
TO_FAR_NEAR = [(b, (b + 2 if b % 2 == 0 else b - 2) % COUNT) for b in range(COUNT)]
TO_FAR_MATE = [(b, (b - 2 if b % 2 == 0 else b + 2) % COUNT) for b in range(COUNT)]
EVEN_UP = [(b, (b + 2) % COUNT if b % 2 == 0 else b) for b in range(COUNT)]


def along_y(shift):
    return [(a, ((a // 2 + shift) % 4) * 2 + a % 2) for a in range(8)]


ACROSS_X = [(a, a ^ 1) for a in range(8)]


def to_upper_even(flip):
    pairs = []
    for b in range(COUNT):
        core = b % 2
        for a in range(8):
            if a % 2 == core ^ flip:
                pairs.append((b * 8 + a, (b - core + 2) % COUNT * 8 + a // 2 * 2 + core))
            else:
                pairs.append((b * 8 + a, (b | 1) * 8 + a))
    return pairs


def f32(*shape):
    return jax.ShapeDtypeStruct(shape, F32)


def parity():
    return lax.rem(lax.axis_index("blk"), 2)


def call(kernel, out_shape, *args, flops=0, scratch=(), specs=None, hidden=(), limit=16):
    single = not isinstance(out_shape, list)
    moved = sum(a.size * a.dtype.itemsize for a in args)
    return pl.pallas_call(
        kernel,
        out_shape=out_shape,
        in_specs=(specs or [VMEM] * len(args)) + [ANY] * len(hidden),
        out_specs=VMEM if single else [VMEM] * len(out_shape),
        scratch_shapes=list(scratch),
        compiler_params=pltpu.CompilerParams(vmem_limit_bytes=limit << 20),
        cost_estimate=pl.CostEstimate(flops=flops, bytes_accessed=moved, transcendentals=0),
    )(*args, *hidden)


def take_kernel(other, first, count, factors, *refs):
    out, sems = refs[-2:]
    odd = parity()
    base = (1 - odd if other else odd) * HALF + first
    copies = [
        pltpu.make_async_copy(factors.at[base + q], out.at[q], sems.at[q]) for q in range(count)
    ]
    for copy in copies:
        copy.start()
    for copy in copies:
        copy.wait()


def take(factors, other, first, count, after=()):
    return call(
        functools.partial(take_kernel, other, first, count),
        jax.ShapeDtypeStruct((count, ROWS, DEPTH), BF16),
        factors,
        scratch=[pltpu.SemaphoreType.DMA((count,))],
        specs=[HBM],
        hidden=after,
        limit=44,
    )


def dot(lo, hi):
    return lax.dot_general(lo, hi, (((1,), (1,)), ((), ())), preferred_element_type=F32)


def accumulate(totals, pairs, first=0, last=HALF):
    totals[...] = jnp.zeros(totals.shape, F32)
    cuts = {first, last}
    for pair in pairs:
        for operand in pair:
            cuts |= {at for _, at in operand if first < at < last}
    cuts = sorted(cuts)

    def holder(operand, at):
        return [piece for piece in operand if piece[1] <= at][-1]

    for low, high in zip(cuts, cuts[1:]):
        held = [[holder(operand, low) for operand in pair] for pair in pairs]

        def step(q, carry):
            for t, ((lo, lo_at), (hi, hi_at)) in enumerate(held):
                totals[t] += dot(lo[q - lo_at], hi[q - hi_at])
            return carry

        lax.fori_loop(low, high, step, 0)


def by_parity(even, odd):
    for which, action in ((0, even), (1, odd)):
        pl.when(parity() == which)(action)


def row_of(shift, height):
    y = lax.div(lax.axis_index("aux"), 2)
    return pl.multiple_of(lax.rem(y + shift, 4) * height, height)


def spread(totals, outs):
    for shift, out in enumerate(outs):
        out[...] = totals[:, pl.ds(row_of(shift, 64), 64)]


def chip_kernel(own0, own1, mate0, *refs):
    outs, totals = refs[:4], refs[4]
    own, mate = [(own0, 0), (own1, CUT)], [(mate0, 0)]
    by_parity(
        lambda: accumulate(totals, [(own, own), (mate, mate), (own, mate)]),
        lambda: accumulate(totals, [(mate, mate), (own, own), (mate, own)]),
    )
    spread(totals, outs)


def window_kernel(own0, own1, mate0, near0, far0, far1, hidden, *refs):
    outs, totals = refs[:4], refs[4]
    own, far = [(own0, 0), (own1, CUT)], [(far0, 0), (far1, CUT)]
    mate, near = [(mate0, 0)], [(near0, 0)]
    by_parity(
        lambda: accumulate(totals, [(near, own), (near, mate), (far, own), (far, mate)]),
        lambda: accumulate(totals, [(own, near), (own, far), (mate, near), (mate, far)]),
    )
    spread(totals, outs)


def sum_kernel(a, b, c, d, total):
    total[...] = a[...] + b[...] + c[...] + d[...]


def choose_kernel(chip, swapped, lower, keep, give):
    def even():
        keep[0] = chip[0]
        keep[1] = lower[0]
        keep[2] = lower[2]
        keep[3] = jnp.zeros((64, ROWS), F32)
        give[0:2] = chip[1:3]
        give[2] = lower[1]
        give[3] = lower[3]

    def odd():
        keep[0:2] = chip[1:3]
        keep[2] = swapped[1]
        keep[3] = swapped[3]
        give[0] = chip[0]
        give[1] = swapped[0]
        give[2] = swapped[2]
        give[3] = jnp.zeros((64, ROWS), F32)

    by_parity(even, odd)


def split_kernel(keep, given, stay, leave):
    pair = lax.rem(lax.axis_index("aux"), 2)
    for half, out in ((pair, stay), (1 - pair, leave)):
        rows = pl.ds(pl.multiple_of(32 * half, 32), 32)
        out[...] = keep[:, rows] + given[:, rows]


def early_kernel(near0, far0, total):
    near, far = [(near0, 0)], [(far0, 0)]
    by_parity(
        lambda: accumulate(total, [(near, far)], 0, CUT),
        lambda: accumulate(total, [(far, near)], 0, CUT),
    )


def last_kernel(near0, far1, early, hidden, keep, give, total):
    near, far = [(near0, 0)], [(far1, CUT)]
    by_parity(
        lambda: accumulate(total, [(near, far)], CUT, HALF),
        lambda: accumulate(total, [(far, near)], CUT, HALF),
    )
    core = parity()
    for y in range(4):
        for half, out in ((core, keep), (1 - core, give)):
            rows = pl.ds(pl.multiple_of(64 * y + 32 * half, 32), 32)
            out[32 * y : 32 * y + 32] = early[0, rows] + total[0, rows]


def combine_last_kernel(keep, given, *outs):
    for shift, out in enumerate(outs):
        rows = pl.ds(row_of(shift, 32), 32)
        out[...] = keep[rows] + given[rows]


def finish_kernel(stay, come, a, b, out):
    out[0:3] = stay[0:3] + come[0:3]
    out[3] = stay[3] + come[3]

    @pl.when(parity() == 0)
    def _():
        out[3] += a[...] + b[...]


def sum_along_y(parts):
    return [parts[0]] + [lax.ppermute(parts[d], "aux", along_y(d)) for d in (1, 2, 3)]


def local(factors):
    def send(value, pairs):
        return lax.ppermute(value, "blk", pairs)

    tile = 2 * ROWS * ROWS * DEPTH
    rest = take(factors, True, 0, HALF)
    near = send(rest, TO_NEAR)
    own = [take(factors, False, CUT, HALF - CUT, (rest,))]
    own.insert(0, take(factors, False, 0, CUT, (own[0],)))
    far_near = [send(part, TO_FAR_NEAR) for part in own]
    far_mate = [send(part, TO_FAR_MATE) for part in own]
    mate = send(rest, TO_MATE)

    parts = call(
        chip_kernel,
        [f32(3, 64, ROWS)] * 4,
        *own,
        mate,
        flops=3 * tile * HALF,
        scratch=[pltpu.VMEM((3, ROWS, ROWS), F32)],
    )
    chip = call(sum_kernel, f32(3, 64, ROWS), *sum_along_y(parts))
    parts = call(
        window_kernel,
        [f32(4, 64, ROWS)] * 4,
        *own,
        mate,
        near,
        *far_near,
        hidden=(chip,),
        flops=4 * tile * HALF,
        scratch=[pltpu.VMEM((4, ROWS, ROWS), F32)],
    )
    window = call(sum_kernel, f32(4, 64, ROWS), *sum_along_y(parts))
    swapped = send(window, TO_MATE)
    lower = send(swapped, EVEN_UP)
    keep, give = call(choose_kernel, [f32(4, 64, ROWS)] * 2, chip, swapped, lower)
    given = send(give, TO_MATE)

    stay, leave = call(split_kernel, [f32(4, 32, ROWS)] * 2, keep, given)
    come = lax.ppermute(leave, "aux", ACROSS_X)

    early = call(
        early_kernel, f32(1, ROWS, ROWS), near, far_mate[0], flops=CUT * tile
    )
    keep_last, give_last = call(
        last_kernel,
        [f32(128, ROWS)] * 2,
        near,
        far_mate[1],
        early,
        hidden=(leave,),
        flops=(HALF - CUT) * tile,
        scratch=[pltpu.VMEM((1, ROWS, ROWS), F32)],
    )
    parts = call(combine_last_kernel, [f32(32, ROWS)] * 4, keep_last, send(give_last, TO_MATE))
    last = call(sum_kernel, f32(32, ROWS), *sum_along_y(parts))
    arrived = [lax.ppermute(last, ("blk", "aux"), to_upper_even(flip)) for flip in (1, 0)]
    out = call(finish_kernel, f32(4, 32, ROWS), stay, come, *arrived)
    return out.transpose(2, 0, 1)


def solution(mesh):
    placed = (P("aux", "blk", None),)
    return jax.shard_map(
        local, mesh=mesh, in_specs=placed, out_specs=P("blk", None, "aux"), check_vma=False
    )
```

```python
import functools

import jax
import jax.numpy as jnp
from jax import lax
from jax.experimental import pallas as pl
from jax.experimental.pallas import tpu as pltpu
from jax.sharding import PartitionSpec as P

COUNT = 32
HALF = 8
CUT = 7
ROWS = 256
DEPTH = 1024
F32 = jnp.float32
BF16 = jnp.bfloat16
ANY = pl.BlockSpec(memory_space=pl.ANY)
HBM = pl.BlockSpec(memory_space=pltpu.HBM)
VMEM = pl.BlockSpec(memory_space=pltpu.VMEM)

TO_MATE = [(b, b ^ 1) for b in range(COUNT)]
TO_NEAR = [(b, (b - 1 if b % 2 == 0 else b + 1) % COUNT) for b in range(COUNT)]
TO_FAR_NEAR = [(b, (b + 2 if b % 2 == 0 else b - 2) % COUNT) for b in range(COUNT)]
TO_FAR_MATE = [(b, (b - 2 if b % 2 == 0 else b + 2) % COUNT) for b in range(COUNT)]


def along_y(shift):
    return [(a, ((a // 2 + shift) % 4) * 2 + a % 2) for a in range(8)]


def by_core(even_shift, odd_shift):
    pairs = []
    for b in range(COUNT):
        moves = along_y(odd_shift if b % 2 else even_shift)
        pairs += [(b * 8 + source, b * 8 + target) for source, target in moves]
    return pairs


ACROSS_X = [(a, a ^ 1) for a in range(8)]


def to_upper_chip():
    pairs = []
    for b in range(COUNT):
        core = b % 2
        for a in range(8):
            block = (b - core + 2 + (core ^ a % 2)) % COUNT
            pairs.append((b * 8 + a, block * 8 + a // 2 * 2 + core))
    return pairs


def f32(*shape):
    return jax.ShapeDtypeStruct(shape, F32)


def parity():
    return lax.rem(lax.axis_index("blk"), 2)


def call(kernel, out_shape, *args, flops=0, scratch=(), specs=None, hidden=(), limit=16):
    single = not isinstance(out_shape, list)
    moved = sum(a.size * a.dtype.itemsize for a in args)
    return pl.pallas_call(
        kernel,
        out_shape=out_shape,
        in_specs=(specs or [VMEM] * len(args)) + [ANY] * len(hidden),
        out_specs=VMEM if single else [VMEM] * len(out_shape),
        scratch_shapes=list(scratch),
        compiler_params=pltpu.CompilerParams(vmem_limit_bytes=limit << 20),
        cost_estimate=pl.CostEstimate(flops=flops, bytes_accessed=moved, transcendentals=0),
    )(*args, *hidden)


def take_kernel(other, first, count, factors, *refs):
    out, sems = refs[-2:]
    odd = parity()
    base = (1 - odd if other else odd) * HALF + first
    copies = [
        pltpu.make_async_copy(factors.at[base + q], out.at[q], sems.at[q]) for q in range(count)
    ]
    for copy in copies:
        copy.start()
    for copy in copies:
        copy.wait()


def take(factors, other, first, count, after=()):
    return call(
        functools.partial(take_kernel, other, first, count),
        jax.ShapeDtypeStruct((count, ROWS, DEPTH), BF16),
        factors,
        scratch=[pltpu.SemaphoreType.DMA((count,))],
        specs=[HBM],
        hidden=after,
        limit=44,
    )


def dot(lo, hi):
    return lax.dot_general(lo, hi, (((1,), (1,)), ((), ())), preferred_element_type=F32)


def accumulate(totals, pairs, first=0, last=HALF):
    totals[...] = jnp.zeros(totals.shape, F32)
    cuts = {first, last}
    for pair in pairs:
        for operand in pair:
            cuts |= {at for _, at in operand if first < at < last}
    cuts = sorted(cuts)

    def holder(operand, at):
        return [piece for piece in operand if piece[1] <= at][-1]

    for low, high in zip(cuts, cuts[1:]):
        held = [[holder(operand, low) for operand in pair] for pair in pairs]

        def step(q, carry):
            for t, ((lo, lo_at), (hi, hi_at)) in enumerate(held):
                totals[t] += dot(lo[q - lo_at], hi[q - hi_at])
            return carry

        lax.fori_loop(low, high, step, 0)


def by_parity(even, odd):
    for which, action in ((0, even), (1, odd)):
        pl.when(parity() == which)(action)


def row_of(shift, height):
    y = lax.div(lax.axis_index("aux"), 2)
    return pl.multiple_of(lax.rem(y + shift, 4) * height, height)


def spread(totals, outs):
    for shift, out in enumerate(outs):
        out[...] = totals[:, pl.ds(row_of(shift, 64), 64)]


def chip_kernel(own0, own1, mate0, *refs):
    outs, totals = refs[:4], refs[4]
    own, mate = [(own0, 0), (own1, CUT)], [(mate0, 0)]
    by_parity(
        lambda: accumulate(totals, [(own, own), (mate, mate), (own, mate)]),
        lambda: accumulate(totals, [(mate, mate), (own, own), (mate, own)]),
    )
    spread(totals, outs)


def window_kernel(own0, own1, mate0, near0, far0, far1, hidden, *refs):
    outs, totals = refs[:4], refs[4]
    own, far = [(own0, 0), (own1, CUT)], [(far0, 0), (far1, CUT)]
    mate, near = [(mate0, 0)], [(near0, 0)]
    by_parity(
        lambda: accumulate(totals, [(near, own), (near, mate), (far, own), (far, mate)]),
        lambda: accumulate(totals, [(own, near), (own, far), (mate, near), (mate, far)]),
    )
    spread(totals, outs)


def sum_kernel(a, b, c, d, total):
    total[...] = a[...] + b[...] + c[...] + d[...]


def choose_kernel(chip, window, keep, give):
    zero = jnp.zeros((64, ROWS), F32)

    def even():
        for slot, tile in enumerate((chip[0], window[0], window[2], zero)):
            keep[slot] = tile
        for slot, tile in enumerate((chip[1], chip[2], window[1], window[3])):
            give[slot] = tile

    def odd():
        for slot, tile in enumerate((chip[1], chip[2], zero, zero)):
            keep[slot] = tile
        give[0] = chip[0]
        for pair in range(2):
            give[1 + pair, 0:32] = window[2 * pair, 0:32]
            give[1 + pair, 32:64] = window[2 * pair + 1, 0:32]
        give[3] = zero

    by_parity(even, odd)


def split_kernel(keep, given, window, stay, leave, up):
    pair = lax.rem(lax.axis_index("aux"), 2)
    mine = pl.ds(pl.multiple_of(32 * pair, 32), 32)
    theirs = pl.ds(pl.multiple_of(32 - 32 * pair, 32), 32)
    for rows, out in ((mine, stay), (theirs, leave)):

        def even():
            out[0] = keep[0, rows] + given[0, rows]
            out[1:4] = keep[1:4, rows]

        def odd():
            out[0:2] = keep[0:2, rows] + given[0:2, rows]
            out[2:4] = given[2:4, rows]

        by_parity(even, odd)

    def up_even():
        for i in range(4):
            first = 32 * (i % 2)
            up[i] = given[1 + i // 2, first : first + 32]

    def up_odd():
        up[...] = window[:, 32:64]

    by_parity(up_even, up_odd)


def early_kernel(near0, far0, total):
    near, far = [(near0, 0)], [(far0, 0)]
    by_parity(
        lambda: accumulate(total, [(near, far)], 0, CUT),
        lambda: accumulate(total, [(far, near)], 0, CUT),
    )


def last_kernel(near0, far1, early, hidden, total):
    near, far = [(near0, 0)], [(far1, CUT)]
    by_parity(
        lambda: accumulate(total, [(near, far)], CUT, HALF),
        lambda: accumulate(total, [(far, near)], CUT, HALF),
    )
    total[...] += early[...]


def combine_last_kernel(mine, given, own, first, second):
    even = parity() == 0
    for shift, out in ((0, own), (jnp.where(even, 1, 2), first), (3, second)):
        rows = pl.ds(row_of(shift, 64), 64)
        out[...] = mine[0, rows] + given[0, rows]


def collect_kernel(own, first, second, keep, give):
    def even():
        total = own[...] + first[...] + second[...]
        keep[...] = total[0:32]
        give[...] = total[32:64]

    def odd():
        keep[...] = first[32:64]
        give[...] = first[0:32]

    by_parity(even, odd)


def join_kernel(a, b, up, hidden, out):
    out[0] = a[...] + b[...]
    for slot, tile in ((1, 0), (2, 2), (3, 1), (4, 3)):
        out[slot] = up[tile]


def hand_kernel(arrived, give):
    def even():
        give[0:2] = arrived[3:5]
        give[2] = jnp.zeros((32, ROWS), F32)

    def odd():
        give[...] = arrived[0:3]

    by_parity(even, odd)


def finish_kernel(stay, come, arrived, given, out):
    def even():
        out[0] = stay[0] + come[0]
        out[1:3] = (stay[1:3] + come[1:3]) + (arrived[1:3] + given[1:3])
        out[3] = arrived[0] + given[0]

    def odd():
        out[0:2] = stay[0:2] + come[0:2]
        out[2:4] = (stay[2:4] + come[2:4]) + (arrived[3:5] + given[0:2])

    by_parity(even, odd)


def sum_along_y(parts):
    return [parts[0]] + [lax.ppermute(parts[d], "aux", along_y(d)) for d in (1, 2, 3)]


def local(factors):
    def send(value, pairs):
        return lax.ppermute(value, "blk", pairs)

    tile = 2 * ROWS * ROWS * DEPTH
    rest = take(factors, True, 0, HALF)
    near = send(rest, TO_NEAR)
    own = [take(factors, False, CUT, HALF - CUT, (rest,))]
    own.insert(0, take(factors, False, 0, CUT, (own[0],)))
    far_near = [send(part, TO_FAR_NEAR) for part in own]
    far_mate = [send(part, TO_FAR_MATE) for part in own]
    mate = send(rest, TO_MATE)

    parts = call(
        chip_kernel,
        [f32(3, 64, ROWS)] * 4,
        *own,
        mate,
        flops=3 * tile * HALF,
        scratch=[pltpu.VMEM((3, ROWS, ROWS), F32)],
    )
    chip = call(sum_kernel, f32(3, 64, ROWS), *sum_along_y(parts))
    parts = call(
        window_kernel,
        [f32(4, 64, ROWS)] * 4,
        *own,
        mate,
        near,
        *far_near,
        hidden=(chip,),
        flops=4 * tile * HALF,
        scratch=[pltpu.VMEM((4, ROWS, ROWS), F32)],
    )
    window = call(sum_kernel, f32(4, 64, ROWS), *sum_along_y(parts))
    keep, give = call(choose_kernel, [f32(4, 64, ROWS)] * 2, chip, window)
    given = send(give, TO_MATE)
    stay, leave, up = call(split_kernel, [f32(4, 32, ROWS)] * 3, keep, given, window)
    come = lax.ppermute(leave, "aux", ACROSS_X)

    early = call(
        early_kernel, f32(1, ROWS, ROWS), near, far_mate[0], flops=CUT * tile
    )
    mine = call(
        last_kernel,
        f32(1, ROWS, ROWS),
        near,
        far_mate[1],
        early,
        hidden=(leave,),
        flops=(HALF - CUT) * tile,
    )
    parts = call(combine_last_kernel, [f32(64, ROWS)] * 3, mine, send(mine, TO_MATE))
    moved = [
        lax.ppermute(part, ("blk", "aux"), by_core(even, odd))
        for part, even, odd in ((parts[1], 1, 2), (parts[2], 3, 3))
    ]
    keep, give = call(collect_kernel, [f32(32, ROWS)] * 2, parts[0], *moved)
    joined = call(join_kernel, f32(5, 32, ROWS), keep, send(give, TO_MATE), up, hidden=(come,))
    arrived = lax.ppermute(joined, ("blk", "aux"), to_upper_chip())
    given = send(call(hand_kernel, f32(3, 32, ROWS), arrived), TO_MATE)
    out = call(finish_kernel, f32(4, 32, ROWS), stay, come, arrived, given)
    return out.transpose(2, 0, 1)


def solution(mesh):
    placed = (P("aux", "blk", None),)
    return jax.shard_map(
        local, mesh=mesh, in_specs=placed, out_specs=P("blk", None, "aux"), check_vma=False
    )
```

```python
import functools

import jax
import jax.numpy as jnp
from jax import lax
from jax.experimental import pallas as pl
from jax.experimental.pallas import tpu as pltpu
from jax.sharding import PartitionSpec as P

COUNT = 32
HALF = 8
CUT = 7
ROWS = 256
DEPTH = 1024
F32 = jnp.float32
BF16 = jnp.bfloat16
ANY = pl.BlockSpec(memory_space=pl.ANY)
HBM = pl.BlockSpec(memory_space=pltpu.HBM)
VMEM = pl.BlockSpec(memory_space=pltpu.VMEM)

TO_MATE = [(b, b ^ 1) for b in range(COUNT)]
TO_NEAR = [(b, (b - 1 if b % 2 == 0 else b + 1) % COUNT) for b in range(COUNT)]
TO_FAR_NEAR = [(b, (b + 2 if b % 2 == 0 else b - 2) % COUNT) for b in range(COUNT)]
TO_FAR_MATE = [(b, (b - 2 if b % 2 == 0 else b + 2) % COUNT) for b in range(COUNT)]


def along_y(shift):
    return [(a, ((a // 2 + shift) % 4) * 2 + a % 2) for a in range(8)]


def by_core(even_shift, odd_shift):
    pairs = []
    for b in range(COUNT):
        moves = along_y(odd_shift if b % 2 else even_shift)
        pairs += [(b * 8 + source, b * 8 + target) for source, target in moves]
    return pairs


ACROSS_X = [(a, a ^ 1) for a in range(8)]


def to_upper_chip():
    pairs = []
    for b in range(COUNT):
        core = b % 2
        for a in range(8):
            block = (b - core + 2 + (core ^ a % 2)) % COUNT
            pairs.append((b * 8 + a, block * 8 + a // 2 * 2 + core))
    return pairs


def f32(*shape):
    return jax.ShapeDtypeStruct(shape, F32)


def parity():
    return lax.rem(lax.axis_index("blk"), 2)


def call(kernel, out_shape, *args, flops=0, scratch=(), specs=None, hidden=(), limit=16):
    single = not isinstance(out_shape, list)
    moved = sum(a.size * a.dtype.itemsize for a in args)
    return pl.pallas_call(
        kernel,
        out_shape=out_shape,
        in_specs=(specs or [VMEM] * len(args)) + [ANY] * len(hidden),
        out_specs=VMEM if single else [VMEM] * len(out_shape),
        scratch_shapes=list(scratch),
        compiler_params=pltpu.CompilerParams(vmem_limit_bytes=limit << 20),
        cost_estimate=pl.CostEstimate(flops=flops, bytes_accessed=moved, transcendentals=0),
    )(*args, *hidden)


def take_kernel(other, first, count, factors, *refs):
    out, sems = refs[-2:]
    odd = parity()
    base = (1 - odd if other else odd) * HALF + first
    copies = [
        pltpu.make_async_copy(factors.at[base + q], out.at[q], sems.at[q]) for q in range(count)
    ]
    for copy in copies:
        copy.start()
    for copy in copies:
        copy.wait()


def take(factors, other, first, count, after=()):
    return call(
        functools.partial(take_kernel, other, first, count),
        jax.ShapeDtypeStruct((count, ROWS, DEPTH), BF16),
        factors,
        scratch=[pltpu.SemaphoreType.DMA((count,))],
        specs=[HBM],
        hidden=after,
        limit=44,
    )


def dot(lo, hi):
    return lax.dot_general(lo, hi, (((1,), (1,)), ((), ())), preferred_element_type=F32)


def accumulate(totals, pairs, first=0, last=HALF):
    totals[...] = jnp.zeros(totals.shape, F32)
    cuts = {first, last}
    for pair in pairs:
        for operand in pair:
            cuts |= {at for _, at in operand if first < at < last}
    cuts = sorted(cuts)

    def holder(operand, at):
        return [piece for piece in operand if piece[1] <= at][-1]

    for low, high in zip(cuts, cuts[1:]):
        held = [[holder(operand, low) for operand in pair] for pair in pairs]

        def step(q, carry):
            for t, ((lo, lo_at), (hi, hi_at)) in enumerate(held):
                totals[t] += dot(lo[q - lo_at], hi[q - hi_at])
            return carry

        lax.fori_loop(low, high, step, 0)


def by_parity(even, odd):
    for which, action in ((0, even), (1, odd)):
        pl.when(parity() == which)(action)


def row_of(shift, height):
    y = lax.div(lax.axis_index("aux"), 2)
    return pl.multiple_of(lax.rem(y + shift, 4) * height, height)


def spread(totals, outs):
    for shift, out in enumerate(outs):
        out[...] = totals[:, pl.ds(row_of(shift, 64), 64)]


def chip_kernel(own0, own1, mate0, *refs):
    outs, totals = refs[:4], refs[4]
    own, mate = [(own0, 0), (own1, CUT)], [(mate0, 0)]
    by_parity(
        lambda: accumulate(totals, [(own, own), (mate, mate), (own, mate)]),
        lambda: accumulate(totals, [(mate, mate), (own, own), (mate, own)]),
    )
    spread(totals, outs)


def window_kernel(own0, own1, mate0, near0, far0, far1, hidden, *refs):
    outs, totals = refs[:4], refs[4]
    own, far = [(own0, 0), (own1, CUT)], [(far0, 0), (far1, CUT)]
    mate, near = [(mate0, 0)], [(near0, 0)]
    by_parity(
        lambda: accumulate(totals, [(near, own), (near, mate), (far, own), (far, mate)]),
        lambda: accumulate(totals, [(own, near), (own, far), (mate, near), (mate, far)]),
    )
    spread(totals, outs)


def sum_kernel(a, b, c, d, total):
    total[...] = a[...] + b[...] + c[...] + d[...]


def choose_kernel(chip, window, keep, give):
    zero = jnp.zeros((64, ROWS), F32)

    def even():
        for slot, tile in enumerate((chip[0], window[0], window[2], zero)):
            keep[slot] = tile
        for slot, tile in enumerate((chip[1], chip[2], window[1], window[3])):
            give[slot] = tile

    def odd():
        for slot, tile in enumerate((chip[1], chip[2], zero, zero)):
            keep[slot] = tile
        give[0] = chip[0]
        for pair in range(2):
            give[1 + pair, 0:32] = window[2 * pair, 0:32]
            give[1 + pair, 32:64] = window[2 * pair + 1, 0:32]
        give[3] = zero

    by_parity(even, odd)


def split_kernel(keep, given, window, stay, leave, up):
    pair = lax.rem(lax.axis_index("aux"), 2)
    mine = pl.ds(pl.multiple_of(32 * pair, 32), 32)
    theirs = pl.ds(pl.multiple_of(32 - 32 * pair, 32), 32)
    for rows, out in ((mine, stay), (theirs, leave)):

        def even():
            out[0] = keep[0, rows] + given[0, rows]
            out[1:4] = keep[1:4, rows]

        def odd():
            out[0:2] = keep[0:2, rows] + given[0:2, rows]
            out[2:4] = given[2:4, rows]

        by_parity(even, odd)

    def up_even():
        for i in range(4):
            first = 32 * (i % 2)
            up[i] = given[1 + i // 2, first : first + 32]

    def up_odd():
        up[...] = window[:, 32:64]

    by_parity(up_even, up_odd)


def early_kernel(near0, far0, total):
    near, far = [(near0, 0)], [(far0, 0)]
    by_parity(
        lambda: accumulate(total, [(near, far)], 0, CUT),
        lambda: accumulate(total, [(far, near)], 0, CUT),
    )


def last_kernel(near0, far1, early, hidden, total):
    near, far = [(near0, 0)], [(far1, CUT)]
    by_parity(
        lambda: accumulate(total, [(near, far)], CUT, HALF),
        lambda: accumulate(total, [(far, near)], CUT, HALF),
    )
    total[...] += early[...]


def combine_last_kernel(mine, given, own, first, second):
    even = parity() == 0
    for shift, out in ((0, own), (jnp.where(even, 1, 2), first), (3, second)):
        rows = pl.ds(row_of(shift, 64), 64)
        out[...] = mine[0, rows] + given[0, rows]


def collect_kernel(own, first, second, keep, give):
    def even():
        total = own[...] + first[...] + second[...]
        keep[...] = total[0:32]
        give[...] = total[32:64]

    def odd():
        keep[...] = first[32:64]
        give[...] = first[0:32]

    by_parity(even, odd)


def join_kernel(a, b, hidden, out):
    out[...] = a[...] + b[...]


def hand_kernel(last, up, give):
    def even():
        give[0] = up[1]
        give[1] = up[3]
        give[2] = jnp.zeros((32, ROWS), F32)

    def odd():
        give[0] = up[0]
        give[1] = up[2]
        give[2] = last[...]

    by_parity(even, odd)


def finish_kernel(stay, come, last, up, given, out):
    def even():
        out[0] = stay[0] + come[0]
        out[1] = (stay[1] + come[1]) + (up[0] + given[0])
        out[2] = (stay[2] + come[2]) + (up[2] + given[1])
        out[3] = last[...] + given[2]

    def odd():
        out[0:2] = stay[0:2] + come[0:2]
        out[2] = (stay[2] + come[2]) + (up[1] + given[0])
        out[3] = (stay[3] + come[3]) + (up[3] + given[1])

    by_parity(even, odd)


def sum_along_y(parts):
    return [parts[0]] + [lax.ppermute(parts[d], "aux", along_y(d)) for d in (1, 2, 3)]


def local(factors):
    def send(value, pairs):
        return lax.ppermute(value, "blk", pairs)

    tile = 2 * ROWS * ROWS * DEPTH
    rest = take(factors, True, 0, HALF)
    near = send(rest, TO_NEAR)
    own = [take(factors, False, CUT, HALF - CUT, (rest,))]
    own.insert(0, take(factors, False, 0, CUT, (own[0],)))
    far_near = [send(part, TO_FAR_NEAR) for part in own]
    far_mate = [send(part, TO_FAR_MATE) for part in own]
    mate = send(rest, TO_MATE)

    parts = call(
        chip_kernel,
        [f32(3, 64, ROWS)] * 4,
        *own,
        mate,
        flops=3 * tile * HALF,
        scratch=[pltpu.VMEM((3, ROWS, ROWS), F32)],
    )
    chip = call(sum_kernel, f32(3, 64, ROWS), *sum_along_y(parts))
    parts = call(
        window_kernel,
        [f32(4, 64, ROWS)] * 4,
        *own,
        mate,
        near,
        *far_near,
        hidden=(chip,),
        flops=4 * tile * HALF,
        scratch=[pltpu.VMEM((4, ROWS, ROWS), F32)],
    )
    window = call(sum_kernel, f32(4, 64, ROWS), *sum_along_y(parts))
    keep, give = call(choose_kernel, [f32(4, 64, ROWS)] * 2, chip, window)
    given = send(give, TO_MATE)
    stay, leave, up = call(split_kernel, [f32(4, 32, ROWS)] * 3, keep, given, window)
    come = lax.ppermute(leave, "aux", ACROSS_X)

    early = call(
        early_kernel, f32(1, ROWS, ROWS), near, far_mate[0], flops=CUT * tile
    )
    mine = call(
        last_kernel,
        f32(1, ROWS, ROWS),
        near,
        far_mate[1],
        early,
        hidden=(leave,),
        flops=(HALF - CUT) * tile,
    )
    parts = call(combine_last_kernel, [f32(64, ROWS)] * 3, mine, send(mine, TO_MATE))
    moved = [
        lax.ppermute(part, ("blk", "aux"), by_core(even, odd))
        for part, even, odd in ((parts[1], 1, 2), (parts[2], 3, 3))
    ]
    keep, give = call(collect_kernel, [f32(32, ROWS)] * 2, parts[0], *moved)
    up = lax.ppermute(up, ("blk", "aux"), to_upper_chip())
    last = call(join_kernel, f32(32, ROWS), keep, send(give, TO_MATE), hidden=(up,))
    last = lax.ppermute(last, ("blk", "aux"), to_upper_chip())
    given = send(call(hand_kernel, f32(3, 32, ROWS), last, up), TO_MATE)
    out = call(finish_kernel, f32(4, 32, ROWS), stay, come, last, up, given)
    return out.transpose(2, 0, 1)


def solution(mesh):
    placed = (P("aux", "blk", None),)
    return jax.shard_map(
        local, mesh=mesh, in_specs=placed, out_specs=P("blk", None, "aux"), check_vma=False
    )
```

```python
import functools

import jax
import jax.numpy as jnp
from jax import lax
from jax.experimental import pallas as pl
from jax.experimental.pallas import tpu as pltpu
from jax.sharding import PartitionSpec as P

COUNT = 32
HALF = 8
CUT = 7
ROWS = 256
DEPTH = 1024
F32 = jnp.float32
BF16 = jnp.bfloat16
ANY = pl.BlockSpec(memory_space=pl.ANY)
HBM = pl.BlockSpec(memory_space=pltpu.HBM)
VMEM = pl.BlockSpec(memory_space=pltpu.VMEM)

TO_MATE = [(b, b ^ 1) for b in range(COUNT)]
TO_NEAR = [(b, (b - 1 if b % 2 == 0 else b + 1) % COUNT) for b in range(COUNT)]
TO_FAR_NEAR = [(b, (b + 2 if b % 2 == 0 else b - 2) % COUNT) for b in range(COUNT)]
TO_FAR_MATE = [(b, (b - 2 if b % 2 == 0 else b + 2) % COUNT) for b in range(COUNT)]


def along_y(shift):
    return [(a, ((a // 2 + shift) % 4) * 2 + a % 2) for a in range(8)]


def by_core(even_shift, odd_shift):
    pairs = []
    for b in range(COUNT):
        moves = along_y(odd_shift if b % 2 else even_shift)
        pairs += [(b * 8 + source, b * 8 + target) for source, target in moves]
    return pairs


ACROSS_X = [(a, a ^ 1) for a in range(8)]


def to_upper_chip():
    pairs = []
    for b in range(COUNT):
        core = b % 2
        for a in range(8):
            block = (b - core + 2 + (core ^ a % 2)) % COUNT
            pairs.append((b * 8 + a, block * 8 + a // 2 * 2 + core))
    return pairs


def to_upper_even(flip):
    pairs = []
    for b in range(COUNT):
        core = b % 2
        for a in range(8):
            if a % 2 == core ^ flip:
                target = (b - core + 2) % COUNT * 8 + a // 2 * 2 + core
            elif core == 0:
                target = (b + 1) * 8 + a
            else:
                target = b * 8 + (a + 2) % 8
            pairs.append((b * 8 + a, target))
    return pairs


def f32(*shape):
    return jax.ShapeDtypeStruct(shape, F32)


def parity():
    return lax.rem(lax.axis_index("blk"), 2)


def call(kernel, out_shape, *args, flops=0, scratch=(), specs=None, hidden=(), limit=16):
    single = not isinstance(out_shape, list)
    moved = sum(a.size * a.dtype.itemsize for a in args)
    return pl.pallas_call(
        kernel,
        out_shape=out_shape,
        in_specs=(specs or [VMEM] * len(args)) + [ANY] * len(hidden),
        out_specs=VMEM if single else [VMEM] * len(out_shape),
        scratch_shapes=list(scratch),
        compiler_params=pltpu.CompilerParams(vmem_limit_bytes=limit << 20),
        cost_estimate=pl.CostEstimate(flops=flops, bytes_accessed=moved, transcendentals=0),
    )(*args, *hidden)


def take_kernel(other, first, count, factors, *refs):
    out, sems = refs[-2:]
    odd = parity()
    base = (1 - odd if other else odd) * HALF + first
    copies = [
        pltpu.make_async_copy(factors.at[base + q], out.at[q], sems.at[q]) for q in range(count)
    ]
    for copy in copies:
        copy.start()
    for copy in copies:
        copy.wait()


def take(factors, other, first, count, after=()):
    return call(
        functools.partial(take_kernel, other, first, count),
        jax.ShapeDtypeStruct((count, ROWS, DEPTH), BF16),
        factors,
        scratch=[pltpu.SemaphoreType.DMA((count,))],
        specs=[HBM],
        hidden=after,
        limit=44,
    )


def dot(lo, hi):
    return lax.dot_general(lo, hi, (((1,), (1,)), ((), ())), preferred_element_type=F32)


def accumulate(totals, pairs, first=0, last=HALF):
    totals[...] = jnp.zeros(totals.shape, F32)
    cuts = {first, last}
    for pair in pairs:
        for operand in pair:
            cuts |= {at for _, at in operand if first < at < last}
    cuts = sorted(cuts)

    def holder(operand, at):
        return [piece for piece in operand if piece[1] <= at][-1]

    for low, high in zip(cuts, cuts[1:]):
        held = [[holder(operand, low) for operand in pair] for pair in pairs]

        def step(q, carry):
            for t, ((lo, lo_at), (hi, hi_at)) in enumerate(held):
                totals[t] += dot(lo[q - lo_at], hi[q - hi_at])
            return carry

        lax.fori_loop(low, high, step, 0)


def by_parity(even, odd):
    for which, action in ((0, even), (1, odd)):
        pl.when(parity() == which)(action)


def row_of(shift, height):
    y = lax.div(lax.axis_index("aux"), 2)
    return pl.multiple_of(lax.rem(y + shift, 4) * height, height)


def spread(totals, outs):
    for shift, out in enumerate(outs):
        out[...] = totals[:, pl.ds(row_of(shift, 64), 64)]


def chip_kernel(own0, own1, mate0, *refs):
    outs, totals = refs[:4], refs[4]
    own, mate = [(own0, 0), (own1, CUT)], [(mate0, 0)]
    by_parity(
        lambda: accumulate(totals, [(own, own), (mate, mate), (own, mate)]),
        lambda: accumulate(totals, [(mate, mate), (own, own), (mate, own)]),
    )
    spread(totals, outs)


def window_kernel(own0, own1, mate0, near0, far0, far1, hidden, *refs):
    outs, totals = refs[:4], refs[4]
    own, far = [(own0, 0), (own1, CUT)], [(far0, 0), (far1, CUT)]
    mate, near = [(mate0, 0)], [(near0, 0)]
    by_parity(
        lambda: accumulate(totals, [(near, own), (near, mate), (far, own), (far, mate)]),
        lambda: accumulate(totals, [(own, near), (own, far), (mate, near), (mate, far)]),
    )
    spread(totals, outs)


def sum_kernel(a, b, c, d, total):
    total[...] = a[...] + b[...] + c[...] + d[...]


def choose_kernel(chip, window, keep, give):
    zero = jnp.zeros((64, ROWS), F32)

    def even():
        for slot, tile in enumerate((chip[0], window[0], window[2], zero)):
            keep[slot] = tile
        for slot, tile in enumerate((chip[1], chip[2], window[1], window[3])):
            give[slot] = tile

    def odd():
        for slot, tile in enumerate((chip[1], chip[2], zero, zero)):
            keep[slot] = tile
        give[0] = chip[0]
        for pair in range(2):
            give[1 + pair, 0:32] = window[2 * pair, 0:32]
            give[1 + pair, 32:64] = window[2 * pair + 1, 0:32]
        give[3] = zero

    by_parity(even, odd)


def split_kernel(keep, given, window, stay, leave, up):
    pair = lax.rem(lax.axis_index("aux"), 2)
    mine = pl.ds(pl.multiple_of(32 * pair, 32), 32)
    theirs = pl.ds(pl.multiple_of(32 - 32 * pair, 32), 32)
    for rows, out in ((mine, stay), (theirs, leave)):

        def even():
            out[0] = keep[0, rows] + given[0, rows]
            out[1:4] = keep[1:4, rows]

        def odd():
            out[0:2] = keep[0:2, rows] + given[0:2, rows]
            out[2:4] = given[2:4, rows]

        by_parity(even, odd)

    def up_even():
        for i in range(4):
            first = 32 * (i % 2)
            up[i] = given[1 + i // 2, first : first + 32]

    def up_odd():
        up[...] = window[:, 32:64]

    by_parity(up_even, up_odd)


def early_kernel(near0, far0, total):
    near, far = [(near0, 0)], [(far0, 0)]
    by_parity(
        lambda: accumulate(total, [(near, far)], 0, CUT),
        lambda: accumulate(total, [(far, near)], 0, CUT),
    )


def last_kernel(near0, far1, early, hidden, total):
    near, far = [(near0, 0)], [(far1, CUT)]
    by_parity(
        lambda: accumulate(total, [(near, far)], CUT, HALF),
        lambda: accumulate(total, [(far, near)], CUT, HALF),
    )
    total[...] += early[...]


def combine_last_kernel(mine, given, own, first, second):
    even = parity() == 0
    for shift, out in ((0, own), (jnp.where(even, 1, 2), first), (3, second)):
        rows = pl.ds(row_of(shift, 64), 64)
        out[...] = mine[0, rows] + given[0, rows]


def collect_kernel(own, first, second, keep, give):
    def even():
        total = own[...] + first[...] + second[...]
        keep[...] = total[0:32]
        give[...] = total[32:64]

    def odd():
        keep[...] = first[32:64]
        give[...] = first[0:32]

    by_parity(even, odd)


def join_kernel(a, b, hidden, out):
    out[...] = a[...] + b[...]


def hand_kernel(up, give):
    def even():
        give[0] = up[1]
        give[1] = up[3]

    def odd():
        give[0] = up[0]
        give[1] = up[2]

    by_parity(even, odd)


def finish_kernel(stay, come, up, given, first, second, out):
    def even():
        out[0] = stay[0] + come[0]
        out[1] = (stay[1] + come[1]) + (up[0] + given[0])
        out[2] = (stay[2] + come[2]) + (up[2] + given[1])
        out[3] = first[...] + second[...]

    def odd():
        out[0:2] = stay[0:2] + come[0:2]
        out[2] = (stay[2] + come[2]) + (up[1] + given[0])
        out[3] = (stay[3] + come[3]) + (up[3] + given[1])

    by_parity(even, odd)


def sum_along_y(parts):
    return [parts[0]] + [lax.ppermute(parts[d], "aux", along_y(d)) for d in (1, 2, 3)]


def local(factors):
    def send(value, pairs):
        return lax.ppermute(value, "blk", pairs)

    tile = 2 * ROWS * ROWS * DEPTH
    rest = take(factors, True, 0, HALF)
    near = send(rest, TO_NEAR)
    own = [take(factors, False, CUT, HALF - CUT, (rest,))]
    own.insert(0, take(factors, False, 0, CUT, (own[0],)))
    far_near = [send(part, TO_FAR_NEAR) for part in own]
    far_mate = [send(part, TO_FAR_MATE) for part in own]
    mate = send(rest, TO_MATE)

    parts = call(
        chip_kernel,
        [f32(3, 64, ROWS)] * 4,
        *own,
        mate,
        flops=3 * tile * HALF,
        scratch=[pltpu.VMEM((3, ROWS, ROWS), F32)],
    )
    chip = call(sum_kernel, f32(3, 64, ROWS), *sum_along_y(parts))
    parts = call(
        window_kernel,
        [f32(4, 64, ROWS)] * 4,
        *own,
        mate,
        near,
        *far_near,
        hidden=(chip,),
        flops=4 * tile * HALF,
        scratch=[pltpu.VMEM((4, ROWS, ROWS), F32)],
    )
    window = call(sum_kernel, f32(4, 64, ROWS), *sum_along_y(parts))
    keep, give = call(choose_kernel, [f32(4, 64, ROWS)] * 2, chip, window)
    given = send(give, TO_MATE)
    stay, leave, up = call(split_kernel, [f32(4, 32, ROWS)] * 3, keep, given, window)
    come = lax.ppermute(leave, "aux", ACROSS_X)

    early = call(
        early_kernel, f32(1, ROWS, ROWS), near, far_mate[0], flops=CUT * tile
    )
    mine = call(
        last_kernel,
        f32(1, ROWS, ROWS),
        near,
        far_mate[1],
        early,
        hidden=(leave,),
        flops=(HALF - CUT) * tile,
    )
    parts = call(combine_last_kernel, [f32(64, ROWS)] * 3, mine, send(mine, TO_MATE))
    moved = [
        lax.ppermute(part, ("blk", "aux"), by_core(even, odd))
        for part, even, odd in ((parts[1], 1, 2), (parts[2], 3, 3))
    ]
    keep, give = call(collect_kernel, [f32(32, ROWS)] * 2, parts[0], *moved)
    up = lax.ppermute(up, ("blk", "aux"), to_upper_chip())
    last = call(join_kernel, f32(32, ROWS), keep, send(give, TO_MATE), hidden=(up,))
    last = [lax.ppermute(last, ("blk", "aux"), to_upper_even(flip)) for flip in (1, 0)]
    given = send(call(hand_kernel, f32(2, 32, ROWS), up), TO_MATE)
    out = call(finish_kernel, f32(4, 32, ROWS), stay, come, up, given, *last)
    return out.transpose(2, 0, 1)


def solution(mesh):
    placed = (P("aux", "blk", None),)
    return jax.shard_map(
        local, mesh=mesh, in_specs=placed, out_specs=P("blk", None, "aux"), check_vma=False
    )
```

```python
import functools

import jax
import jax.numpy as jnp
from jax import lax
from jax.experimental import pallas as pl
from jax.experimental.pallas import tpu as pltpu
from jax.sharding import PartitionSpec as P

COUNT = 32
HALF = 8
CUT = 7
ROWS = 256
DEPTH = 1024
F32 = jnp.float32
BF16 = jnp.bfloat16
ANY = pl.BlockSpec(memory_space=pl.ANY)
HBM = pl.BlockSpec(memory_space=pltpu.HBM)
VMEM = pl.BlockSpec(memory_space=pltpu.VMEM)

TO_MATE = [(b, b ^ 1) for b in range(COUNT)]
TO_NEAR = [(b, (b - 1 if b % 2 == 0 else b + 1) % COUNT) for b in range(COUNT)]
TO_FAR_NEAR = [(b, (b + 2 if b % 2 == 0 else b - 2) % COUNT) for b in range(COUNT)]
TO_FAR_MATE = [(b, (b - 2 if b % 2 == 0 else b + 2) % COUNT) for b in range(COUNT)]


def along_y(shift):
    return [(a, ((a // 2 + shift) % 4) * 2 + a % 2) for a in range(8)]


def by_core(even_shift, odd_shift):
    pairs = []
    for b in range(COUNT):
        moves = along_y(odd_shift if b % 2 else even_shift)
        pairs += [(b * 8 + source, b * 8 + target) for source, target in moves]
    return pairs


ACROSS_X = [(a, a ^ 1) for a in range(8)]


def to_upper_chip():
    pairs = []
    for b in range(COUNT):
        core = b % 2
        for a in range(8):
            block = (b - core + 2 + (core ^ a % 2)) % COUNT
            pairs.append((b * 8 + a, block * 8 + a // 2 * 2 + core))
    return pairs


def to_upper_even(from_core):
    pairs = []
    for b in range(COUNT):
        core = b % 2
        for a in range(8):
            if from_core == 0:
                target = (b + 2) % COUNT * 8 + a if core == 0 else b * 8 + (a + 2) % 8
            else:
                target = (b + 1) % COUNT * 8 + (a ^ 1 if core == 1 else a)
            pairs.append((b * 8 + a, target))
    return pairs


def f32(*shape):
    return jax.ShapeDtypeStruct(shape, F32)


def parity():
    return lax.rem(lax.axis_index("blk"), 2)


def call(kernel, out_shape, *args, flops=0, scratch=(), specs=None, hidden=(), limit=16):
    single = not isinstance(out_shape, list)
    moved = sum(a.size * a.dtype.itemsize for a in args)
    return pl.pallas_call(
        kernel,
        out_shape=out_shape,
        in_specs=(specs or [VMEM] * len(args)) + [ANY] * len(hidden),
        out_specs=VMEM if single else [VMEM] * len(out_shape),
        scratch_shapes=list(scratch),
        compiler_params=pltpu.CompilerParams(vmem_limit_bytes=limit << 20),
        cost_estimate=pl.CostEstimate(flops=flops, bytes_accessed=moved, transcendentals=0),
    )(*args, *hidden)


def take_kernel(other, first, count, factors, *refs):
    out, sems = refs[-2:]
    odd = parity()
    base = (1 - odd if other else odd) * HALF + first
    copies = [
        pltpu.make_async_copy(factors.at[base + q], out.at[q], sems.at[q]) for q in range(count)
    ]
    for copy in copies:
        copy.start()
    for copy in copies:
        copy.wait()


def take(factors, other, first, count, after=()):
    return call(
        functools.partial(take_kernel, other, first, count),
        jax.ShapeDtypeStruct((count, ROWS, DEPTH), BF16),
        factors,
        scratch=[pltpu.SemaphoreType.DMA((count,))],
        specs=[HBM],
        hidden=after,
        limit=44,
    )


def dot(lo, hi):
    return lax.dot_general(lo, hi, (((1,), (1,)), ((), ())), preferred_element_type=F32)


def accumulate(totals, pairs, first=0, last=HALF):
    totals[...] = jnp.zeros(totals.shape, F32)
    cuts = {first, last}
    for pair in pairs:
        for operand in pair:
            cuts |= {at for _, at in operand if first < at < last}
    cuts = sorted(cuts)

    def holder(operand, at):
        return [piece for piece in operand if piece[1] <= at][-1]

    for low, high in zip(cuts, cuts[1:]):
        held = [[holder(operand, low) for operand in pair] for pair in pairs]

        def step(q, carry):
            for t, ((lo, lo_at), (hi, hi_at)) in enumerate(held):
                totals[t] += dot(lo[q - lo_at], hi[q - hi_at])
            return carry

        lax.fori_loop(low, high, step, 0)


def by_parity(even, odd):
    for which, action in ((0, even), (1, odd)):
        pl.when(parity() == which)(action)


def row_of(shift, height):
    y = lax.div(lax.axis_index("aux"), 2)
    return pl.multiple_of(lax.rem(y + shift, 4) * height, height)


def spread(totals, outs):
    for shift, out in enumerate(outs):
        out[...] = totals[:, pl.ds(row_of(shift, 64), 64)]


def chip_kernel(own0, own1, mate0, *refs):
    outs, totals = refs[:4], refs[4]
    own, mate = [(own0, 0), (own1, CUT)], [(mate0, 0)]
    by_parity(
        lambda: accumulate(totals, [(own, own), (mate, mate), (own, mate)]),
        lambda: accumulate(totals, [(mate, mate), (own, own), (mate, own)]),
    )
    spread(totals, outs)


def window_kernel(own0, own1, mate0, near0, far0, far1, hidden, *refs):
    outs, totals = refs[:4], refs[4]
    own, far = [(own0, 0), (own1, CUT)], [(far0, 0), (far1, CUT)]
    mate, near = [(mate0, 0)], [(near0, 0)]
    by_parity(
        lambda: accumulate(totals, [(near, own), (near, mate), (far, own), (far, mate)]),
        lambda: accumulate(totals, [(own, near), (own, far), (mate, near), (mate, far)]),
    )
    spread(totals, outs)


def sum_kernel(a, b, c, d, total):
    total[...] = a[...] + b[...] + c[...] + d[...]


def choose_kernel(chip, window, keep, give):
    zero = jnp.zeros((64, ROWS), F32)

    def even():
        for slot, tile in enumerate((chip[0], window[0], window[2], zero)):
            keep[slot] = tile
        for slot, tile in enumerate((chip[1], chip[2], window[1], window[3])):
            give[slot] = tile

    def odd():
        for slot, tile in enumerate((chip[1], chip[2], zero, zero)):
            keep[slot] = tile
        give[0] = chip[0]
        for pair in range(2):
            give[1 + pair, 0:32] = window[2 * pair, 0:32]
            give[1 + pair, 32:64] = window[2 * pair + 1, 0:32]
        give[3] = zero

    by_parity(even, odd)


def split_kernel(keep, given, window, stay, leave, up):
    pair = lax.rem(lax.axis_index("aux"), 2)
    mine = pl.ds(pl.multiple_of(32 * pair, 32), 32)
    theirs = pl.ds(pl.multiple_of(32 - 32 * pair, 32), 32)
    for rows, out in ((mine, stay), (theirs, leave)):

        def even():
            out[0] = keep[0, rows] + given[0, rows]
            out[1:4] = keep[1:4, rows]

        def odd():
            out[0:2] = keep[0:2, rows] + given[0:2, rows]
            out[2:4] = given[2:4, rows]

        by_parity(even, odd)

    def up_even():
        for i in range(4):
            first = 32 * (i % 2)
            up[i] = given[1 + i // 2, first : first + 32]

    def up_odd():
        up[...] = window[:, 32:64]

    by_parity(up_even, up_odd)


def early_kernel(near0, far0, total):
    near, far = [(near0, 0)], [(far0, 0)]
    by_parity(
        lambda: accumulate(total, [(near, far)], 0, CUT),
        lambda: accumulate(total, [(far, near)], 0, CUT),
    )


def last_kernel(near0, far1, early, hidden, total):
    near, far = [(near0, 0)], [(far1, CUT)]
    by_parity(
        lambda: accumulate(total, [(near, far)], CUT, HALF),
        lambda: accumulate(total, [(far, near)], CUT, HALF),
    )
    total[...] += early[...]


def combine_last_kernel(mine, given, own, first, second):
    even = parity() == 0
    for shift, out in ((0, own), (jnp.where(even, 1, 2), first), (3, second)):
        rows = pl.ds(row_of(shift, 64), 64)
        out[...] = mine[0, rows] + given[0, rows]


def collect_kernel(own, first, second, keep, give):
    pair = lax.rem(lax.axis_index("aux"), 2)
    same = pl.ds(pl.multiple_of(32 * pair, 32), 32)
    cross = pl.ds(pl.multiple_of(32 - 32 * pair, 32), 32)

    def even():
        keep[...] = own[same] + first[same] + second[same]
        give[...] = own[cross] + first[cross] + second[cross]

    def odd():
        keep[...] = first[cross]
        give[...] = first[same]

    by_parity(even, odd)


def join_kernel(a, b, hidden, out):
    out[...] = a[...] + b[...]


def hand_kernel(up, give):
    def even():
        give[0] = up[1]
        give[1] = up[3]

    def odd():
        give[0] = up[0]
        give[1] = up[2]

    by_parity(even, odd)


def finish_kernel(stay, come, up, given, first, second, out):
    def even():
        out[0] = stay[0] + come[0]
        out[1] = (stay[1] + come[1]) + (up[0] + given[0])
        out[2] = (stay[2] + come[2]) + (up[2] + given[1])
        out[3] = first[...] + second[...]

    def odd():
        out[0:2] = stay[0:2] + come[0:2]
        out[2] = (stay[2] + come[2]) + (up[1] + given[0])
        out[3] = (stay[3] + come[3]) + (up[3] + given[1])

    by_parity(even, odd)


def sum_along_y(parts):
    return [parts[0]] + [lax.ppermute(parts[d], "aux", along_y(d)) for d in (1, 2, 3)]


def local(factors):
    def send(value, pairs):
        return lax.ppermute(value, "blk", pairs)

    tile = 2 * ROWS * ROWS * DEPTH
    rest = take(factors, True, 0, HALF)
    near = send(rest, TO_NEAR)
    own = [take(factors, False, CUT, HALF - CUT, (rest,))]
    own.insert(0, take(factors, False, 0, CUT, (own[0],)))
    far_near = [send(part, TO_FAR_NEAR) for part in own]
    far_mate = [send(part, TO_FAR_MATE) for part in own]
    mate = send(rest, TO_MATE)

    parts = call(
        chip_kernel,
        [f32(3, 64, ROWS)] * 4,
        *own,
        mate,
        flops=3 * tile * HALF,
        scratch=[pltpu.VMEM((3, ROWS, ROWS), F32)],
    )
    chip = call(sum_kernel, f32(3, 64, ROWS), *sum_along_y(parts))
    parts = call(
        window_kernel,
        [f32(4, 64, ROWS)] * 4,
        *own,
        mate,
        near,
        *far_near,
        hidden=(chip,),
        flops=4 * tile * HALF,
        scratch=[pltpu.VMEM((4, ROWS, ROWS), F32)],
    )
    window = call(sum_kernel, f32(4, 64, ROWS), *sum_along_y(parts))
    keep, give = call(choose_kernel, [f32(4, 64, ROWS)] * 2, chip, window)
    given = send(give, TO_MATE)
    stay, leave, up = call(split_kernel, [f32(4, 32, ROWS)] * 3, keep, given, window)
    come = lax.ppermute(leave, "aux", ACROSS_X)

    early = call(
        early_kernel, f32(1, ROWS, ROWS), near, far_mate[0], flops=CUT * tile
    )
    mine = call(
        last_kernel,
        f32(1, ROWS, ROWS),
        near,
        far_mate[1],
        early,
        hidden=(leave,),
        flops=(HALF - CUT) * tile,
    )
    parts = call(combine_last_kernel, [f32(64, ROWS)] * 3, mine, send(mine, TO_MATE))
    moved = [
        lax.ppermute(part, ("blk", "aux"), by_core(even, odd))
        for part, even, odd in ((parts[1], 1, 2), (parts[2], 3, 3))
    ]
    keep, give = call(collect_kernel, [f32(32, ROWS)] * 2, parts[0], *moved)
    up = lax.ppermute(up, ("blk", "aux"), to_upper_chip())
    last = call(join_kernel, f32(32, ROWS), keep, send(give, TO_MATE), hidden=(up,))
    last = [lax.ppermute(last, ("blk", "aux"), to_upper_even(core)) for core in (1, 0)]
    given = send(call(hand_kernel, f32(2, 32, ROWS), up), TO_MATE)
    out = call(finish_kernel, f32(4, 32, ROWS), stay, come, up, given, *last)
    return out.transpose(2, 0, 1)


def solution(mesh):
    placed = (P("aux", "blk", None),)
    return jax.shard_map(
        local, mesh=mesh, in_specs=placed, out_specs=P("blk", None, "aux"), check_vma=False
    )
```

```python
import functools

import jax
import jax.numpy as jnp
from jax import lax
from jax.experimental import pallas as pl
from jax.experimental.pallas import tpu as pltpu
from jax.sharding import PartitionSpec as P

COUNT = 32
HALF = 8
CUT = 7
ROWS = 256
DEPTH = 1024
F32 = jnp.float32
BF16 = jnp.bfloat16
ANY = pl.BlockSpec(memory_space=pl.ANY)
HBM = pl.BlockSpec(memory_space=pltpu.HBM)
VMEM = pl.BlockSpec(memory_space=pltpu.VMEM)

TO_MATE = [(b, b ^ 1) for b in range(COUNT)]
TO_NEAR = [(b, (b - 1 if b % 2 == 0 else b + 1) % COUNT) for b in range(COUNT)]
TO_FAR_NEAR = [(b, (b + 2 if b % 2 == 0 else b - 2) % COUNT) for b in range(COUNT)]
TO_FAR_MATE = [(b, (b - 2 if b % 2 == 0 else b + 2) % COUNT) for b in range(COUNT)]


def along_y(shift):
    return [(a, ((a // 2 + shift) % 4) * 2 + a % 2) for a in range(8)]


def by_core(even_shift, odd_shift):
    pairs = []
    for b in range(COUNT):
        moves = along_y(odd_shift if b % 2 else even_shift)
        pairs += [(b * 8 + source, b * 8 + target) for source, target in moves]
    return pairs


ACROSS_X = [(a, a ^ 1) for a in range(8)]


def to_upper_chip():
    pairs = []
    for b in range(COUNT):
        core = b % 2
        for a in range(8):
            block = (b - core + 2 + (core ^ a % 2)) % COUNT
            pairs.append((b * 8 + a, block * 8 + a // 2 * 2 + core))
    return pairs


def to_upper_even(from_core):
    pairs = []
    for b in range(COUNT):
        core = b % 2
        for a in range(8):
            if from_core == 0:
                target = (b + 2) % COUNT * 8 + a if core == 0 else b * 8 + (a + 2) % 8
            else:
                target = (b + 1) % COUNT * 8 + (a ^ 1 if core == 1 else a)
            pairs.append((b * 8 + a, target))
    return pairs


def f32(*shape):
    return jax.ShapeDtypeStruct(shape, F32)


def parity():
    return lax.rem(lax.axis_index("blk"), 2)


def call(kernel, out_shape, *args, flops=0, scratch=(), specs=None, hidden=(), limit=16):
    single = not isinstance(out_shape, list)
    moved = sum(a.size * a.dtype.itemsize for a in args)
    return pl.pallas_call(
        kernel,
        out_shape=out_shape,
        in_specs=(specs or [VMEM] * len(args)) + [ANY] * len(hidden),
        out_specs=VMEM if single else [VMEM] * len(out_shape),
        scratch_shapes=list(scratch),
        compiler_params=pltpu.CompilerParams(vmem_limit_bytes=limit << 20),
        cost_estimate=pl.CostEstimate(flops=flops, bytes_accessed=moved, transcendentals=0),
    )(*args, *hidden)


def take_kernel(other, first, count, factors, *refs):
    out, sems = refs[-2:]
    odd = parity()
    base = (1 - odd if other else odd) * HALF + first
    copies = [
        pltpu.make_async_copy(factors.at[base + q], out.at[q], sems.at[q]) for q in range(count)
    ]
    for copy in copies:
        copy.start()
    for copy in copies:
        copy.wait()


def take(factors, other, first, count, after=()):
    return call(
        functools.partial(take_kernel, other, first, count),
        jax.ShapeDtypeStruct((count, ROWS, DEPTH), BF16),
        factors,
        scratch=[pltpu.SemaphoreType.DMA((count,))],
        specs=[HBM],
        hidden=after,
        limit=44,
    )


def dot(lo, hi):
    return lax.dot_general(lo, hi, (((1,), (1,)), ((), ())), preferred_element_type=F32)


def accumulate(totals, pairs, first=0, last=HALF):
    totals[...] = jnp.zeros(totals.shape, F32)
    cuts = {first, last}
    for pair in pairs:
        for operand in pair:
            cuts |= {at for _, at in operand if first < at < last}
    cuts = sorted(cuts)

    def holder(operand, at):
        return [piece for piece in operand if piece[1] <= at][-1]

    for low, high in zip(cuts, cuts[1:]):
        held = [[holder(operand, low) for operand in pair] for pair in pairs]

        def step(q, carry):
            for t, ((lo, lo_at), (hi, hi_at)) in enumerate(held):
                totals[t] += dot(lo[q - lo_at], hi[q - hi_at])
            return carry

        lax.fori_loop(low, high, step, 0)


def by_parity(even, odd):
    for which, action in ((0, even), (1, odd)):
        pl.when(parity() == which)(action)


def row_of(shift, height):
    y = lax.div(lax.axis_index("aux"), 2)
    return pl.multiple_of(lax.rem(y + shift, 4) * height, height)


def spread(totals, outs):
    for shift, out in enumerate(outs):
        out[...] = totals[:, pl.ds(row_of(shift, 64), 64)]


def chip_kernel(own0, own1, mate0, *refs):
    outs, totals = refs[:4], refs[4]
    own, mate = [(own0, 0), (own1, CUT)], [(mate0, 0)]
    by_parity(
        lambda: accumulate(totals, [(own, own), (mate, mate), (own, mate)]),
        lambda: accumulate(totals, [(mate, mate), (own, own), (mate, own)]),
    )
    spread(totals, outs)


def window_kernel(own0, own1, mate0, near0, far0, far1, hidden, *refs):
    outs, totals = refs[:4], refs[4]
    own, far = [(own0, 0), (own1, CUT)], [(far0, 0), (far1, CUT)]
    mate, near = [(mate0, 0)], [(near0, 0)]
    by_parity(
        lambda: accumulate(totals, [(near, own), (near, mate), (far, own), (far, mate)]),
        lambda: accumulate(totals, [(own, near), (own, far), (mate, near), (mate, far)]),
    )
    spread(totals, outs)


def sum_kernel(a, b, c, d, total):
    total[...] = a[...] + b[...] + c[...] + d[...]


def choose_kernel(chip, window, keep, give):
    zero = jnp.zeros((64, ROWS), F32)

    def even():
        for slot, tile in enumerate((chip[0], window[0], window[2], zero)):
            keep[slot] = tile
        for slot, tile in enumerate((chip[1], chip[2], window[1], window[3])):
            give[slot] = tile

    def odd():
        for slot, tile in enumerate((chip[1], chip[2], zero, zero)):
            keep[slot] = tile
        give[0] = chip[0]
        for pair in range(2):
            give[1 + pair, 0:32] = window[2 * pair, 0:32]
            give[1 + pair, 32:64] = window[2 * pair + 1, 0:32]
        give[3] = zero

    by_parity(even, odd)


def split_kernel(keep, given, window, stay, leave, up):
    pair = lax.rem(lax.axis_index("aux"), 2)
    mine = pl.ds(pl.multiple_of(32 * pair, 32), 32)
    theirs = pl.ds(pl.multiple_of(32 - 32 * pair, 32), 32)
    for rows, out in ((mine, stay), (theirs, leave)):

        def even():
            out[0] = keep[0, rows] + given[0, rows]
            out[1:4] = keep[1:4, rows]

        def odd():
            out[0:2] = keep[0:2, rows] + given[0:2, rows]
            out[2:4] = given[2:4, rows]

        by_parity(even, odd)

    def up_even():
        for i in range(4):
            first = 32 * (i % 2)
            up[i] = given[1 + i // 2, first : first + 32]

    def up_odd():
        up[...] = window[:, 32:64]

    by_parity(up_even, up_odd)


def early_kernel(near0, far0, total):
    near, far = [(near0, 0)], [(far0, 0)]
    by_parity(
        lambda: accumulate(total, [(near, far)], 0, CUT),
        lambda: accumulate(total, [(far, near)], 0, CUT),
    )


def last_kernel(near0, far1, early, hidden, total):
    near, far = [(near0, 0)], [(far1, CUT)]
    by_parity(
        lambda: accumulate(total, [(near, far)], CUT, HALF),
        lambda: accumulate(total, [(far, near)], CUT, HALF),
    )
    total[...] += early[...]


def combine_last_kernel(mine, given, own, first, second):
    even = parity() == 0
    for shift, out in ((0, own), (jnp.where(even, 1, 2), first), (3, second)):
        rows = pl.ds(row_of(shift, 64), 64)
        out[...] = mine[0, rows] + given[0, rows]


def collect_kernel(own, first, second, keep, give):
    pair = lax.rem(lax.axis_index("aux"), 2)
    same = pl.ds(pl.multiple_of(32 * pair, 32), 32)
    cross = pl.ds(pl.multiple_of(32 - 32 * pair, 32), 32)

    def even():
        keep[...] = own[same] + first[same] + second[same]
        give[...] = own[cross] + first[cross] + second[cross]

    def odd():
        keep[...] = first[cross]
        give[...] = first[same]

    by_parity(even, odd)


def join_kernel(a, b, hidden, out):
    out[...] = a[...] + b[...]


def hand_kernel(up, hidden, give):
    def even():
        give[0] = up[1]
        give[1] = up[3]

    def odd():
        give[0] = up[0]
        give[1] = up[2]

    by_parity(even, odd)


def finish_kernel(stay, come, up, given, first, second, out):
    def even():
        out[0] = stay[0] + come[0]
        out[1] = (stay[1] + come[1]) + (up[0] + given[0])
        out[2] = (stay[2] + come[2]) + (up[2] + given[1])
        out[3] = first[...] + second[...]

    def odd():
        out[0:2] = stay[0:2] + come[0:2]
        out[2] = (stay[2] + come[2]) + (up[1] + given[0])
        out[3] = (stay[3] + come[3]) + (up[3] + given[1])

    by_parity(even, odd)


def sum_along_y(parts):
    return [parts[0]] + [lax.ppermute(parts[d], "aux", along_y(d)) for d in (1, 2, 3)]


def local(factors):
    def send(value, pairs):
        return lax.ppermute(value, "blk", pairs)

    tile = 2 * ROWS * ROWS * DEPTH
    rest = take(factors, True, 0, HALF)
    near = send(rest, TO_NEAR)
    own = [take(factors, False, CUT, HALF - CUT, (rest,))]
    own.insert(0, take(factors, False, 0, CUT, (own[0],)))
    far_near = [send(part, TO_FAR_NEAR) for part in own]
    far_mate = [send(part, TO_FAR_MATE) for part in own]
    mate = send(rest, TO_MATE)

    parts = call(
        chip_kernel,
        [f32(3, 64, ROWS)] * 4,
        *own,
        mate,
        flops=3 * tile * HALF,
        scratch=[pltpu.VMEM((3, ROWS, ROWS), F32)],
    )
    chip = call(sum_kernel, f32(3, 64, ROWS), *sum_along_y(parts))
    parts = call(
        window_kernel,
        [f32(4, 64, ROWS)] * 4,
        *own,
        mate,
        near,
        *far_near,
        hidden=(chip,),
        flops=4 * tile * HALF,
        scratch=[pltpu.VMEM((4, ROWS, ROWS), F32)],
    )
    window = call(sum_kernel, f32(4, 64, ROWS), *sum_along_y(parts))
    keep, give = call(choose_kernel, [f32(4, 64, ROWS)] * 2, chip, window)
    given = send(give, TO_MATE)
    stay, leave, up = call(split_kernel, [f32(4, 32, ROWS)] * 3, keep, given, window)
    come = lax.ppermute(leave, "aux", ACROSS_X)

    early = call(
        early_kernel, f32(1, ROWS, ROWS), near, far_mate[0], flops=CUT * tile
    )
    mine = call(
        last_kernel,
        f32(1, ROWS, ROWS),
        near,
        far_mate[1],
        early,
        hidden=(leave,),
        flops=(HALF - CUT) * tile,
    )
    parts = call(combine_last_kernel, [f32(64, ROWS)] * 3, mine, send(mine, TO_MATE))
    moved = [
        lax.ppermute(part, ("blk", "aux"), by_core(even, odd))
        for part, even, odd in ((parts[1], 1, 2), (parts[2], 3, 3))
    ]
    keep, give = call(collect_kernel, [f32(32, ROWS)] * 2, parts[0], *moved)
    up = lax.ppermute(up, ("blk", "aux"), to_upper_chip())
    joined = call(join_kernel, f32(32, ROWS), keep, send(give, TO_MATE), hidden=(up,))
    last = [lax.ppermute(joined, ("blk", "aux"), to_upper_even(core)) for core in (1, 0)]
    given = send(call(hand_kernel, f32(2, 32, ROWS), up, hidden=(joined,)), TO_MATE)
    out = call(finish_kernel, f32(4, 32, ROWS), stay, come, up, given, *last)
    return out.transpose(2, 0, 1)


def solution(mesh):
    placed = (P("aux", "blk", None),)
    return jax.shard_map(
        local, mesh=mesh, in_specs=placed, out_specs=P("blk", None, "aux"), check_vma=False
    )
```
